32 devices in a mesh: groups: 2 (over x), mp: 8 (over z, y), batch: 2 (over core).
Axes of the slice: x: 2, y: 2, z: 4, core: 2. Of those that a mesh axis runs over, the one named last changes fastest.
Arguments:
- gate_act: bfloat16 [2048, 26624], P(('groups', 'batch'), 'mp'), parts along dimension 0, may hold values from -6 to 6
- up_act: bfloat16 [2048, 26624], P(('groups', 'batch'), 'mp'), parts along dimension 0, may hold values from -6 to 6
- down_weight: bfloat16 [26624, 8, 1024], P('mp', None, 'batch'), may hold values from -0.0546875 to 0.0546875
Outputs:
- layer_out: bfloat16 [2048, 8192], P(('groups', 'batch'), 'mp'), parts along dimension 0
The draws below stay inside these ranges and needn't reach their ends.
There are 2 independent parts, one for each index of `groups`. The reference program is written for one: setup_inputs(seed, part) draws one part's arguments, and reference() takes and returns one part's arrays. A program takes and returns all parts, laid end to end along the dimension named above; an argument that names none is the same for every part. Nothing has to cross between parts.
All inputs are finite; a program needn't handle non-finite values.
Results may differ from the reference program's by a relative error of at most 0.005.
Values may be sent and summed in bfloat16 or wider, within the bound.
No kernel may reach another device: no remote copies, remote signals or barrier semaphores. Data moves between devices by JAX's collectives and lax.ppermute only.
A program may use at most 320 MiB of HBM per device.

```python
import jax
import jax.numpy as jnp

DMODEL = 8192
HIDDEN_UNITS = 26624
ROWS = 1024
N_MP = 8


def strengthened(values, own_key, source, target, blocks, factor):
    def block_of(dim):
        return (jnp.arange(values.shape[dim]) // (values.shape[dim] // blocks)).reshape((-1,) + (1,) * (values.ndim - 1 - dim))

    near = jax.random.permutation(own_key, blocks)[block_of(target)]
    far = (block_of(target) + blocks // 2) % blocks
    return jnp.where((block_of(source) == near) | (block_of(source) == far), factor * values, values)


def block_levels(key, shape, cuts, smallest, top_value):
    def one(position, parts):
        steps = jax.random.uniform(jax.random.fold_in(jax.random.fold_in(key, 6), position), (parts,), jnp.float32, smallest / len(cuts), top_value / len(cuts))
        return jnp.repeat(jnp.exp(steps), shape[position] // parts).reshape((-1,) + (1,) * (len(shape) - position - 1))

    gain = one(*cuts[0])
    for cut in cuts[1:]:
        gain = gain * one(*cut)
    return gain


def normal_values(own_key, shape, scale, limit, shards=(), held_as=jnp.bfloat16):
    drawn = jax.random.normal(own_key, shape, jnp.float32) * scale
    if len(shards) > 0:
        drawn = block_levels(own_key, shape, shards, -0.22, 0.18) * drawn
    return jnp.clip(drawn, min=-limit, max=limit).astype(held_as)


def noise_with(stream_key, dims, deviation, reach, split, heavy, dtype=jnp.bfloat16):
    entries = deviation * jax.random.normal(stream_key, dims, jnp.float32)
    if split:
        entries = entries * block_levels(stream_key, dims, split, -0.22, 0.18)
    return jnp.clip(strengthened(entries, jax.random.fold_in(stream_key, 3), *heavy), -reach, reach).astype(dtype)


def setup_inputs(seed: int = 0, part: int = 0) -> dict:
    key_of = jax.random.split(jax.random.key(seed), 4)
    own_keys = jax.random.split(jax.random.fold_in(key_of[3], part), 4)
    return {
        "gate_act": normal_values(own_keys[0], (ROWS, HIDDEN_UNITS), 1.0, 6.0, ((0, 2), (1, 8))),
        "up_act": normal_values(own_keys[1], (ROWS, HIDDEN_UNITS), 1.0, 6.0, ((0, 2), (1, 8))),
        "down_weight": noise_with(key_of[2], (HIDDEN_UNITS, N_MP, DMODEL // N_MP), HIDDEN_UNITS ** -0.5, 0.0546875, ((0, 8), (2, 2)), (0, 1, 8, 2.0)),
    }


def reference(gate_act, up_act, down_weight):
    hidden = (jax.nn.silu(gate_act.astype(jnp.float32)) * up_act.astype(jnp.float32)).astype(jnp.bfloat16)
    matrix = down_weight.reshape(down_weight.shape[0], -1)
    return jnp.dot(hidden, matrix, preferred_element_type=jnp.float32).astype(jnp.bfloat16)
```

```python
import functools

import jax
import jax.numpy as jnp
from jax import lax
from jax.experimental import pallas as pl
from jax.experimental.pallas import tpu as pltpu
from jax.sharding import PartitionSpec as P

LANES = 128
SLAB = 256
SLABS = 8
VMEM_LIMIT = 56 * 1024 * 1024


def gated(gate_act, up_act):
    return (jax.nn.silu(gate_act.astype(jnp.float32)) * up_act.astype(jnp.float32)).astype(
        jnp.bfloat16
    )


def product_kernel(n_hid, pairs, n_after, w_ref, *refs):
    hid_refs, refs = refs[:n_hid], refs[n_hid + n_after:]
    out_refs, (order, w_sorted, hid, sems) = refs[:-4], refs[-4:]
    step = pl.program_id(0)
    depth = w_sorted.shape[1]
    sort_steps = depth * 8 // (SLAB * SLABS)
    rows = hid_refs[0].shape[0]
    per = SLAB // 8

    def copies():
        return [
            pltpu.make_async_copy(h, hid.at[pl.ds(n * rows, rows)], sems.at[n]) for n, h in enumerate(hid_refs)
        ]

    @pl.when(step == 0)
    def _():
        for c in copies():
            c.start()
        me = lax.axis_index("mp")
        z, y = me // 2, me % 2
        to = lax.broadcasted_iota(jnp.int32, (SLAB, SLAB), 0)
        at = lax.broadcasted_iota(jnp.int32, (SLAB, SLAB), 1)
        block = at % 8
        place = ((block % 2 + y + 1) % 2) * 4 + (block // 2 - z + 4) % 4
        same = jnp.logical_and(to % per == at // 8, to // per == place)
        order[...] = jnp.where(same, 1.0, 0.0).astype(jnp.bfloat16)

    @pl.when(step < sort_steps)
    def _():
        for s in range(0, SLABS, 2):
            two = jnp.concatenate(
                [w_ref[s * SLAB:(s + 1) * SLAB, :], w_ref[(s + 1) * SLAB:(s + 2) * SLAB, :]], axis=1
            )
            t = jnp.dot(order[...], two, preferred_element_type=jnp.float32).astype(jnp.bfloat16)
            for half in range(2):
                base = pl.multiple_of((step * SLABS + s + half) * per, per)
                for n, p in enumerate(pairs):
                    for side in range(2):
                        i = p * 2 + side
                        w_sorted[n, pl.ds(base, per), side * LANES:(side + 1) * LANES] = t[
                            i * per:(i + 1) * per, half * LANES:(half + 1) * LANES
                        ]

    @pl.when(step == sort_steps)
    def _():
        for c in copies():
            c.wait()

    for n in range(len(pairs)):
        @pl.when(step == sort_steps + n)
        def _(n=n):
            t = jnp.dot(hid[...], w_sorted[n], preferred_element_type=jnp.float32).astype(jnp.bfloat16)
            out_refs[n // 2][0] = t[:, :LANES]
            out_refs[n // 2][1] = t[:, LANES:]


def products(hids, w2, chunk, pairs, after=()):
    rows = hids[0].shape[0] * len(hids)
    depth = w2.shape[0] // 8
    sort_steps = depth * 8 // (SLAB * SLABS)
    n_out = len(pairs) // 2

    def out_map(o):
        return lambda s: (jnp.clip(s - sort_steps - 2 * o, 0, 1), 0, 0)

    out = pl.pallas_call(
        functools.partial(product_kernel, len(hids), pairs, len(after)),
        grid=(sort_steps + len(pairs),),
        in_specs=[pl.BlockSpec((SLAB * SLABS, LANES), lambda s: (jnp.minimum(s, sort_steps - 1), chunk))]
        + [pl.BlockSpec(memory_space=pl.ANY)] * (len(hids) + len(after)),
        out_specs=[pl.BlockSpec((2, rows, LANES), out_map(o)) for o in range(n_out)],
        out_shape=[jax.ShapeDtypeStruct((4, rows, LANES), jnp.bfloat16)] * n_out,
        scratch_shapes=[
            pltpu.VMEM((SLAB, SLAB), jnp.bfloat16),
            pltpu.VMEM((len(pairs), depth, 2 * LANES), jnp.bfloat16),
            pltpu.VMEM((rows, depth), jnp.bfloat16),
            pltpu.SemaphoreType.DMA((len(hids),)),
        ],
        compiler_params=pltpu.CompilerParams(vmem_limit_bytes=VMEM_LIMIT),
        cost_estimate=pl.CostEstimate(
            flops=2 * rows * depth * len(pairs) * 256 + 2 * depth * 8 * 256 * LANES,
            bytes_accessed=2 * depth * (rows + 8 * LANES), transcendentals=0,
        ),
    )(w2, *hids, *after)
    return out


def combine_kernel(own_ref, got_ref, *out_refs):
    for i in range(4):
        out_refs[i][...] = (own_ref[i].astype(jnp.float32) + got_ref[i].astype(jnp.float32)).astype(jnp.bfloat16)


def combine(own, got):
    _, rows, lanes = own.shape
    step = rows // 4
    spec = pl.BlockSpec((4, step, lanes), lambda r: (0, r, 0))
    return pl.pallas_call(
        combine_kernel,
        grid=(4,),
        in_specs=[spec, spec],
        out_specs=[pl.BlockSpec((step, lanes), lambda r: (r, 0))] * 4,
        out_shape=[jax.ShapeDtypeStruct((rows, lanes), jnp.bfloat16)] * 4,
        cost_estimate=pl.CostEstimate(flops=4 * rows * lanes, bytes_accessed=24 * rows * lanes, transcendentals=0),
    )(own, got)


def add(*terms):
    return sum(t.astype(jnp.float32) for t in terms).astype(jnp.bfloat16)


Y_SWAP = [(i, i ^ 1) for i in range(8)]
PAIR = [(0, 1), (1, 0)]


def along_z(shift):
    return [(i, (i + 2 * shift) % 8) for i in range(8)]


def staged(gate_act, up_act, down_weight):
    batch = lax.axis_index("batch")
    depth, _, width = down_weight.shape
    w2 = down_weight.reshape(depth * 8, width)
    own = gated(gate_act, up_act)
    peer = lax.ppermute(own, "batch", PAIR)
    n_rows = own.shape[0]

    def finish(outward, kept):
        s = combine(kept, lax.ppermute(outward, "mp", Y_SWAP))
        return add(s[0], *[lax.ppermute(s[i], "mp", along_z(i)) for i in (1, 2, 3)])

    (a_out,) = products([own], w2, 0, (0, 1))
    c_out, c_kept = products([peer], w2, 0, (0, 1, 2, 3), (a_out,))
    (a_kept,) = products([own], w2, 0, (2, 3), (c_out,))
    d_out, d_kept = products([own, peer], w2, 1, (0, 1, 2, 3), (a_kept,))
    e_out, e_kept = products([own, peer], w2, 2, (0, 1, 2, 3), (d_out,))
    f_out, f_kept = products([peer], w2, 3, (0, 1, 2, 3), (e_out,))
    g_out, g_kept = products([own], w2, 3, (0, 1, 2, 3), (f_out,))
    a, c = finish(a_out, a_kept), finish(c_out, c_kept)
    d, e = finish(d_out, d_kept), finish(e_out, e_kept)
    f, g = finish(f_out, f_kept), finish(g_out, g_kept)
    mine = jnp.concatenate([a, d[:n_rows], e[:n_rows], g], axis=1)
    theirs = [c, d[n_rows:], e[n_rows:], f]
    got = jnp.concatenate([lax.ppermute(t, "batch", PAIR) for t in theirs], axis=1)
    return jnp.where(batch == 0, jnp.concatenate([mine, got], 1), jnp.concatenate([got, mine], 1))


def general(gate_act, up_act, down_weight):
    hidden = gated(gate_act, up_act)
    piece = lax.all_gather(down_weight, "batch", axis=2, tiled=True)
    flat = piece.reshape(piece.shape[0], -1)
    result = jnp.dot(hidden, flat, preferred_element_type=jnp.float32)
    summed = lax.psum_scatter(result, "mp", scatter_dimension=1, tiled=True)
    return summed.astype(jnp.bfloat16)


def solution(mesh):
    def local(gate_act, up_act, down_weight):
        depth, blocks, width = down_weight.shape
        fits = (
            mesh.shape["mp"] == 8 and blocks == 8 and mesh.shape["batch"] == 2 and width == 4 * LANES
            and depth * 8 % (SLAB * SLABS) == 0
        )
        return (staged if fits else general)(gate_act, up_act, down_weight)

    placed = (P(("groups", "batch"), "mp"), P(("groups", "batch"), "mp"), P("mp", None, "batch"))
    return jax.shard_map(
        local, mesh=mesh, in_specs=placed, out_specs=P(("groups", "batch"), "mp"), check_vma=False
    )
```

```python
import functools

import jax
import jax.numpy as jnp
from jax import lax
from jax.experimental import pallas as pl
from jax.experimental.pallas import tpu as pltpu
from jax.sharding import PartitionSpec as P

LANES = 128
SLAB = 256
SORT_STEPS = 4
COST = 20_000_000_000
STEP_COST = pl.CostEstimate(flops=COST, bytes_accessed=1024, transcendentals=0)
VMEM_LIMIT = 30 * 1024 * 1024


def gated(gate_act, up_act):
    return (jax.nn.silu(gate_act.astype(jnp.float32)) * up_act.astype(jnp.float32)).astype(
        jnp.bfloat16
    )


def product_kernel(n_hid, pairs, n_after, keep, w_ref, *refs):
    hid_refs, refs = refs[:n_hid], refs[n_hid + n_after:]
    out_refs, (order, w_sorted, hid, sems) = refs[:-4], refs[-4:]
    step = pl.program_id(0)
    slabs = w_ref.shape[0] // SLAB
    rows = hid_refs[0].shape[0]
    per = SLAB // 8
    n_sorted = w_sorted.shape[0]

    def copies():
        return [
            pltpu.make_async_copy(h, hid.at[pl.ds(n * rows, rows)], sems.at[n]) for n, h in enumerate(hid_refs)
        ]

    def keeping():
        return pltpu.make_async_copy(w_sorted, out_refs[-1], sems.at[n_hid])

    @pl.when(step == 0)
    def _():
        for c in copies():
            c.start()
        me = lax.axis_index("mp")
        to = lax.broadcasted_iota(jnp.int32, (SLAB, SLAB), 0)
        at = lax.broadcasted_iota(jnp.int32, (SLAB, SLAB), 1)
        block = at % 8
        far, near = (block // 4 + me // 4) % 2, (block // 2 + me // 2 + 1) % 2
        place = ((block % 2 + me + 1) % 2) * 4 + near * 2 + far
        same = jnp.logical_and(to % per == at // 8, to // per == place)
        order[...] = jnp.where(same, 1.0, 0.0).astype(jnp.bfloat16)

    @pl.when(step < SORT_STEPS)
    def _():
        for s in range(0, slabs, 2):
            two = jnp.concatenate(
                [w_ref[s * SLAB:(s + 1) * SLAB, :], w_ref[(s + 1) * SLAB:(s + 2) * SLAB, :]], axis=1
            )
            t = jnp.dot(order[...], two, preferred_element_type=jnp.float32).astype(jnp.bfloat16)
            for half in range(2):
                base = pl.multiple_of((step * slabs + s + half) * per, per)
                for i in range(8):
                    w_sorted[i // 2, pl.ds(base, per), (i % 2) * LANES:(i % 2 + 1) * LANES] = t[
                        i * per:(i + 1) * per, half * LANES:(half + 1) * LANES
                    ]

    @pl.when(step == SORT_STEPS)
    def _():
        if keep:
            keeping().start()
        for c in copies():
            c.wait()

    for n, p in enumerate(pairs):
        @pl.when(step == SORT_STEPS + n)
        def _(n=n, p=p):
            t = jnp.dot(hid[...], w_sorted[p], preferred_element_type=jnp.float32).astype(jnp.bfloat16)
            out_refs[n // 2][0] = t[:, :LANES]
            out_refs[n // 2][1] = t[:, LANES:]
            if keep and n == len(pairs) - 1:
                keeping().wait()


def products(hids, w2, chunk, pairs, after=(), keep=False):
    rows = hids[0].shape[0] * len(hids)
    depth = w2.shape[0] // 8
    n_out = len(pairs) // 2

    def out_map(o):
        return lambda s: (jnp.clip(s - SORT_STEPS - 2 * o, 0, 1), 0, 0)

    kept = jax.ShapeDtypeStruct((4, depth, 2 * LANES), jnp.bfloat16)
    return pl.pallas_call(
        functools.partial(product_kernel, len(hids), pairs, len(after), keep),
        grid=(SORT_STEPS + len(pairs),),
        in_specs=[pl.BlockSpec((depth * 8 // SORT_STEPS, LANES), lambda s: (jnp.minimum(s, SORT_STEPS - 1), chunk))]
        + [pl.BlockSpec(memory_space=pl.ANY)] * (len(hids) + len(after)),
        out_specs=[pl.BlockSpec((2, rows, LANES), out_map(o)) for o in range(n_out)]
        + [pl.BlockSpec(memory_space=pltpu.HBM)] * keep,
        out_shape=[jax.ShapeDtypeStruct((4, rows, LANES), jnp.bfloat16)] * n_out + [kept] * keep,
        scratch_shapes=[
            pltpu.VMEM((SLAB, SLAB), jnp.bfloat16),
            pltpu.VMEM(kept.shape, jnp.bfloat16),
            pltpu.VMEM((rows, depth), jnp.bfloat16),
            pltpu.SemaphoreType.DMA((len(hids) + 1,)),
        ],
        compiler_params=pltpu.CompilerParams(vmem_limit_bytes=VMEM_LIMIT),
        cost_estimate=STEP_COST,
    )(w2, *hids, *after)


def dots_kernel(first, n_pairs, n_after, hid_ref, w_ref, *refs):
    out_refs, (w_held, sems) = refs[n_after:-2], refs[-2:]
    step = pl.program_id(0)

    def copy(n):
        return pltpu.make_async_copy(w_ref.at[first + n], w_held.at[n % 2], sems.at[n % 2])

    for n in range(n_pairs):
        @pl.when(step == n)
        def _(n=n):
            if n == 0:
                copy(0).start()
            if n + 1 < n_pairs:
                copy(n + 1).start()
            copy(n).wait()
            t = jnp.dot(hid_ref[...], w_held[n % 2], preferred_element_type=jnp.float32).astype(jnp.bfloat16)
            out_refs[n // 2][0] = t[:, :LANES]
            out_refs[n // 2][1] = t[:, LANES:]


def dots(hid, w_sorted, first, n_pairs, after=()):
    rows, depth = hid.shape
    n_out = n_pairs // 2

    def out_map(o):
        return lambda s: (jnp.clip(s - 2 * o, 0, 1), 0, 0)

    return pl.pallas_call(
        functools.partial(dots_kernel, first, n_pairs, len(after)),
        grid=(n_pairs,),
        in_specs=[pl.BlockSpec((rows, depth), lambda s: (0, 0)), pl.BlockSpec(memory_space=pltpu.HBM)]
        + [pl.BlockSpec(memory_space=pl.ANY)] * len(after),
        out_specs=[pl.BlockSpec((2, rows, LANES), out_map(o)) for o in range(n_out)],
        out_shape=[jax.ShapeDtypeStruct((4, rows, LANES), jnp.bfloat16)] * n_out,
        scratch_shapes=[pltpu.VMEM((2, depth, 2 * LANES), jnp.bfloat16), pltpu.SemaphoreType.DMA((2,))],
        compiler_params=pltpu.CompilerParams(vmem_limit_bytes=VMEM_LIMIT),
        cost_estimate=STEP_COST,
    )(hid, w_sorted, *after)


def on_vmem(kernel, n_in, after, out_shape, args):
    vmem = pl.BlockSpec(memory_space=pltpu.VMEM)
    many = isinstance(out_shape, list)
    return pl.pallas_call(
        kernel,
        in_specs=[vmem] * n_in + [pl.BlockSpec(memory_space=pl.ANY)] * len(after),
        out_specs=[vmem] * len(out_shape) if many else vmem,
        out_shape=out_shape,
        compiler_params=pltpu.CompilerParams(vmem_limit_bytes=12 * 1024 * 1024),
        cost_estimate=STEP_COST,
    )(*args, *after)


def summed(*refs):
    return sum(r[...].astype(jnp.float32) for r in refs)


def combine_kernel(n_after, own_ref, got_ref, *refs):
    sent, kept = refs[n_after:]
    for i in range(2):
        sent[i] = summed(own_ref.at[i], got_ref.at[i]).astype(jnp.bfloat16)
        kept[i] = summed(own_ref.at[2 + i], got_ref.at[2 + i])


def combine(own, got, after=()):
    _, rows, lanes = own.shape
    shape = [jax.ShapeDtypeStruct((2, rows, lanes), d) for d in (jnp.bfloat16, jnp.float32)]
    return on_vmem(functools.partial(combine_kernel, len(after)), 2, after, shape, (own, got))


def merge_kernel(n_after, own_ref, got_ref, *refs):
    sent, kept = refs[n_after:]
    sent[...] = summed(own_ref.at[1], got_ref.at[1]).astype(jnp.bfloat16)
    kept[...] = summed(own_ref.at[0], got_ref.at[0])


def merge(own, got, after=()):
    _, rows, lanes = own.shape
    shape = [jax.ShapeDtypeStruct((rows, lanes), d) for d in (jnp.bfloat16, jnp.float32)]
    return on_vmem(functools.partial(merge_kernel, len(after)), 2, after, shape, (own, got))


def total_kernel(n_after, parts, own_ref, got_ref, *refs):
    outs = refs[n_after:]
    rows = outs[0].shape[0]
    for p in range(parts):
        at = pl.ds(p * rows, rows)
        outs[p][...] = summed(own_ref.at[at], got_ref.at[at]).astype(jnp.bfloat16)


def total(terms, parts, after=()):
    rows, lanes = terms[0].shape
    shape = [jax.ShapeDtypeStruct((rows // parts, lanes), jnp.bfloat16)] * parts
    return on_vmem(functools.partial(total_kernel, len(after), parts), 2, after, shape, terms)


def whole_kernel(*refs):
    out, mine, theirs, terms = refs[-1], refs[:3], refs[3:7], refs[7:9]
    batch = lax.axis_index("batch")

    for b in range(2):
        @pl.when(batch == b)
        def _(b=b):
            def put(half, n, value):
                at = (half * 4 + n) * LANES
                out[:, at:at + LANES] = value

            for n in range(3):
                put(b, n, mine[n][...])
            put(b, 3, summed(*terms).astype(jnp.bfloat16))
            for n in range(4):
                put(1 - b, n, theirs[n][...])


def whole(mine, theirs, terms):
    rows, lanes = mine[0].shape
    shape = jax.ShapeDtypeStruct((rows, 8 * lanes), jnp.bfloat16)
    return on_vmem(whole_kernel, 9, (), shape, (*mine, *theirs, *terms))


Y_SWAP = [(i, i ^ 1) for i in range(8)]
PAIR = [(0, 1), (1, 0)]


NEAR_SWAP = [(i, i ^ 2) for i in range(8)]
FAR_SWAP = [(i, i ^ 4) for i in range(8)]


def staged(gate_act, up_act, down_weight):
    batch = lax.axis_index("batch")
    depth, _, width = down_weight.shape
    w2 = down_weight.reshape(depth * 8, width)
    own = gated(gate_act, up_act)
    peer = lax.ppermute(own, "batch", PAIR)
    n_rows = own.shape[0]

    def over_y(outward):
        return lax.ppermute(outward, "mp", Y_SWAP)

    last = []

    def step(function, *args):
        result = function(*args, tuple(last))
        last[:] = list(result[:1]) if isinstance(result, (list, tuple)) else [result]
        return result

    def near(kept, got):
        sent, kept = step(combine, kept, got)
        return kept, lax.ppermute(sent, "mp", NEAR_SWAP)

    def far(terms):
        sent, kept = step(merge, *terms)
        return kept, lax.ppermute(sent, "mp", FAR_SWAP)

    def swap(x):
        return lax.ppermute(x, "batch", PAIR)

    every = (0, 1, 2, 3)
    a_out, w0 = products([own], w2, 0, (0, 1), (), True)
    last[:] = [a_out]
    a_got = over_y(a_out)
    c_out, c_kept = step(dots, peer, w0, 0, 4)
    c_got = over_y(c_out)
    d_out, d_kept = step(products, [own, peer], w2, 1, every)
    d_got = over_y(d_out)
    (a_kept,) = step(dots, own, w0, 2, 2)
    a = near(a_kept, a_got)
    c = near(c_kept, c_got)
    e_out, e_kept = step(products, [own, peer], w2, 2, every)
    e_got = over_y(e_out)
    a, c = far(a), far(c)
    f_out, f_kept, w3 = step(lambda *v: products(*v, keep=True), [peer], w2, 3, every)
    f_got = over_y(f_out)
    (a,) = step(total, a, 1)
    d = near(d_kept, d_got)
    g_out, g_kept = step(dots, own, w3, 0, 4)
    g_got = over_y(g_out)
    (c,) = step(total, c, 1)
    d = far(d)
    e = near(e_kept, e_got)
    d_mine, d_theirs = step(total, d, 2)
    f = near(f_kept, f_got)
    e = far(e)
    f = far(f)
    g = near(g_kept, g_got)
    e_mine, e_theirs = step(total, e, 2)
    (f,) = step(total, f, 1)
    g = far(g)
    return whole((a, d_mine, e_mine), [swap(v) for v in (c, d_theirs, e_theirs, f)], g)


def general(gate_act, up_act, down_weight):
    hidden = gated(gate_act, up_act)
    piece = lax.all_gather(down_weight, "batch", axis=2, tiled=True)
    flat = piece.reshape(piece.shape[0], -1)
    result = jnp.dot(hidden, flat, preferred_element_type=jnp.float32)
    summed = lax.psum_scatter(result, "mp", scatter_dimension=1, tiled=True)
    return summed.astype(jnp.bfloat16)


def solution(mesh):
    def local(gate_act, up_act, down_weight):
        depth, blocks, width = down_weight.shape
        fits = (
            mesh.shape["mp"] == 8 and blocks == 8 and mesh.shape["batch"] == 2 and width == 4 * LANES
            and depth * 8 % (2 * SLAB * SORT_STEPS) == 0
        )
        return (staged if fits else general)(gate_act, up_act, down_weight)

    placed = (P(("groups", "batch"), "mp"), P(("groups", "batch"), "mp"), P("mp", None, "batch"))
    return jax.shard_map(
        local, mesh=mesh, in_specs=placed, out_specs=P(("groups", "batch"), "mp"), check_vma=False
    )
```

```python
import functools

import jax
import jax.numpy as jnp
from jax import lax
from jax.experimental import pallas as pl
from jax.experimental.pallas import tpu as pltpu
from jax.sharding import PartitionSpec as P

LANES = 128
SLAB = 256
SORT_STEPS = 4
BIG_STEP = pl.CostEstimate(flops=10_000_000_000, bytes_accessed=1024, transcendentals=0)
SMALL_STEP = pl.CostEstimate(flops=10_000_000_000, bytes_accessed=1024, transcendentals=0)
VMEM_LIMIT = 30 * 1024 * 1024


def gated(gate_act, up_act):
    return (jax.nn.silu(gate_act.astype(jnp.float32)) * up_act.astype(jnp.float32)).astype(
        jnp.bfloat16
    )


def product_kernel(n_hid, pairs, n_after, keep, w_ref, *refs):
    hid_refs, refs = refs[:n_hid], refs[n_hid + n_after:]
    out_refs, (order, w_sorted, hid, sems) = refs[:-4], refs[-4:]
    step = pl.program_id(0)
    slabs = w_ref.shape[0] // SLAB
    rows = hid_refs[0].shape[0]
    per = SLAB // 8
    n_sorted = w_sorted.shape[0]

    def copies():
        return [
            pltpu.make_async_copy(h, hid.at[pl.ds(n * rows, rows)], sems.at[n]) for n, h in enumerate(hid_refs)
        ]

    def keeping():
        return pltpu.make_async_copy(w_sorted.at[pl.ds(4 - keep, keep)], out_refs[-1], sems.at[n_hid])

    @pl.when(step == 0)
    def _():
        for c in copies():
            c.start()
        me = lax.axis_index("mp")
        to = lax.broadcasted_iota(jnp.int32, (SLAB, SLAB), 0)
        at = lax.broadcasted_iota(jnp.int32, (SLAB, SLAB), 1)
        block = at % 8
        far, near = (block // 4 + me // 4) % 2, (block // 2 + me // 2 + 1) % 2
        place = ((block % 2 + me + 1) % 2) * 4 + near * 2 + far
        same = jnp.logical_and(to % per == at // 8, to // per == place)
        order[...] = jnp.where(same, 1.0, 0.0).astype(jnp.bfloat16)

    @pl.when(step < SORT_STEPS)
    def _():
        for s in range(0, slabs, 2):
            two = jnp.concatenate(
                [w_ref[s * SLAB:(s + 1) * SLAB, :], w_ref[(s + 1) * SLAB:(s + 2) * SLAB, :]], axis=1
            )
            t = jnp.dot(order[...], two, preferred_element_type=jnp.float32).astype(jnp.bfloat16)
            for half in range(2):
                base = pl.multiple_of((step * slabs + s + half) * per, per)
                for i in range(8):
                    w_sorted[i // 2, pl.ds(base, per), (i % 2) * LANES:(i % 2 + 1) * LANES] = t[
                        i * per:(i + 1) * per, half * LANES:(half + 1) * LANES
                    ]

    @pl.when(step == SORT_STEPS)
    def _():
        keeping().start()
        for c in copies():
            c.wait()

    for n, p in enumerate(pairs):
        @pl.when(step == SORT_STEPS + n)
        def _(n=n, p=p):
            t = jnp.dot(hid[...], w_sorted[p], preferred_element_type=jnp.float32).astype(jnp.bfloat16)
            out_refs[n // 2][0] = t[:, :LANES]
            out_refs[n // 2][1] = t[:, LANES:]
            if n == len(pairs) - 1:
                keeping().wait()


def products(hids, w2, chunk, pairs, after=(), keep=4):
    rows = hids[0].shape[0] * len(hids)
    depth = w2.shape[0] // 8
    n_out = len(pairs) // 2

    def out_map(o):
        return lambda s: (jnp.clip(s - SORT_STEPS - 2 * o, 0, 1), 0, 0)

    kept = jax.ShapeDtypeStruct((keep, depth, 2 * LANES), jnp.bfloat16)
    return pl.pallas_call(
        functools.partial(product_kernel, len(hids), pairs, len(after), keep),
        grid=(SORT_STEPS + len(pairs),),
        in_specs=[pl.BlockSpec((depth * 8 // SORT_STEPS, LANES), lambda s: (jnp.minimum(s, SORT_STEPS - 1), chunk))]
        + [pl.BlockSpec(memory_space=pl.ANY)] * (len(hids) + len(after)),
        out_specs=[pl.BlockSpec((2, rows, LANES), out_map(o)) for o in range(n_out)]
        + [pl.BlockSpec(memory_space=pltpu.HBM)],
        out_shape=[jax.ShapeDtypeStruct((4, rows, LANES), jnp.bfloat16)] * n_out + [kept],
        scratch_shapes=[
            pltpu.VMEM((SLAB, SLAB), jnp.bfloat16),
            pltpu.VMEM((4, depth, 2 * LANES), jnp.bfloat16),
            pltpu.VMEM((rows, depth), jnp.bfloat16),
            pltpu.SemaphoreType.DMA((len(hids) + 1,)),
        ],
        compiler_params=pltpu.CompilerParams(vmem_limit_bytes=VMEM_LIMIT),
        cost_estimate=BIG_STEP,
    )(w2, *hids, *after)


def dots_kernel(n_hid, pairs, extra, n_after, *refs):
    hid_refs, w_ref, refs = refs[:n_hid], refs[n_hid], refs[n_hid + 1 + n_after:]
    out_refs, (w_held, sems) = refs[:-2], refs[-2:]
    step = pl.program_id(0)
    rows = hid_refs[0].shape[0]

    def copy(n):
        return pltpu.make_async_copy(w_ref.at[pairs[n]], w_held.at[n % 2], sems.at[n % 2])

    def put(hid, n, out, at):
        t = jnp.dot(hid[...], w_held[n % 2], preferred_element_type=jnp.float32).astype(jnp.bfloat16)
        for side in range(2):
            out[side, at:at + rows] = t[:, side * LANES:(side + 1) * LANES]

    for n in range(len(pairs)):
        @pl.when(step == n)
        def _(n=n):
            if n == 0:
                copy(0).start()
            if n + 1 < len(pairs):
                copy(n + 1).start()
            copy(n).wait()
            for h, hid in enumerate(hid_refs):
                if h == 0 or not extra:
                    put(hid, n, out_refs[n // 2], h * rows)
                elif pairs[n] in extra:
                    put(hid, n, out_refs[-1], 0)


def dots(hids, w_sorted, pairs, extra=(), after=()):
    rows, depth = hids[0].shape
    n_out = len(pairs) // 2
    out_rows = rows if extra else rows * len(hids)

    def out_map(o):
        return lambda s: (jnp.clip(s - 2 * o, 0, 1), 0, 0)

    maps = [out_map(o) for o in range(n_out)] + [lambda s: (s // 2, 0, 0)] * bool(extra)
    return pl.pallas_call(
        functools.partial(dots_kernel, len(hids), pairs, extra, len(after)),
        grid=(len(pairs),),
        in_specs=[pl.BlockSpec((rows, depth), lambda s: (0, 0))] * len(hids) + [pl.BlockSpec(memory_space=pltpu.HBM)]
        + [pl.BlockSpec(memory_space=pl.ANY)] * len(after),
        out_specs=[pl.BlockSpec((2, out_rows, LANES), m) for m in maps],
        out_shape=[jax.ShapeDtypeStruct((4, out_rows, LANES), jnp.bfloat16)] * len(maps),
        scratch_shapes=[pltpu.VMEM((2, depth, 2 * LANES), jnp.bfloat16), pltpu.SemaphoreType.DMA((2,))],
        compiler_params=pltpu.CompilerParams(vmem_limit_bytes=VMEM_LIMIT),
        cost_estimate=BIG_STEP,
    )(*hids, w_sorted, *after)


def on_vmem(kernel, n_in, after, out_shape, args):
    vmem = pl.BlockSpec(memory_space=pltpu.VMEM)
    many = isinstance(out_shape, list)
    return pl.pallas_call(
        kernel,
        in_specs=[vmem] * n_in + [pl.BlockSpec(memory_space=pl.ANY)] * len(after),
        out_specs=[vmem] * len(out_shape) if many else vmem,
        out_shape=out_shape,
        compiler_params=pltpu.CompilerParams(vmem_limit_bytes=12 * 1024 * 1024),
        cost_estimate=SMALL_STEP,
    )(*args, *after)


def summed(*refs):
    return sum(r[...].astype(jnp.float32) for r in refs)


def combine_kernel(n_after, own_ref, got_ref, *refs):
    sent, kept = refs[n_after:]
    for i in range(2):
        sent[i] = summed(own_ref.at[i], got_ref.at[i]).astype(jnp.bfloat16)
        kept[i] = summed(own_ref.at[2 + i], got_ref.at[2 + i])


def combine(own, got, after=()):
    _, rows, lanes = own.shape
    shape = [jax.ShapeDtypeStruct((2, rows, lanes), d) for d in (jnp.bfloat16, jnp.float32)]
    return on_vmem(functools.partial(combine_kernel, len(after)), 2, after, shape, (own, got))


def merge_kernel(n_after, own_ref, got_ref, *refs):
    sent, kept = refs[n_after:]
    sent[...] = summed(own_ref.at[1], got_ref.at[1]).astype(jnp.bfloat16)
    kept[...] = summed(own_ref.at[0], got_ref.at[0])


def merge(own, got, after=()):
    _, rows, lanes = own.shape
    shape = [jax.ShapeDtypeStruct((rows, lanes), d) for d in (jnp.bfloat16, jnp.float32)]
    return on_vmem(functools.partial(merge_kernel, len(after)), 2, after, shape, (own, got))


def total_kernel(n_after, parts, own_ref, got_ref, *refs):
    outs = refs[n_after:]
    rows = outs[0].shape[0]
    for p in range(parts):
        at = pl.ds(p * rows, rows)
        outs[p][...] = summed(own_ref.at[at], got_ref.at[at]).astype(jnp.bfloat16)


def total(terms, parts, after=()):
    rows, lanes = terms[0].shape
    shape = [jax.ShapeDtypeStruct((rows // parts, lanes), jnp.bfloat16)] * parts
    return on_vmem(functools.partial(total_kernel, len(after), parts), 2, after, shape, terms)


def whole_kernel(*refs):
    out, mine, theirs, terms = refs[-1], refs[:3], refs[3:7], refs[7:9]
    batch = lax.axis_index("batch")

    for b in range(2):
        @pl.when(batch == b)
        def _(b=b):
            def put(half, n, value):
                out[:, (half * 4 + n) * LANES:(half * 4 + n + 1) * LANES] = value

            for n in range(3):
                put(b, n, mine[n][...])
            put(b, 3, summed(*terms).astype(jnp.bfloat16))
            for n in range(4):
                put(1 - b, n, theirs[n][...])


def whole(mine, theirs, terms):
    rows, lanes = mine[0].shape
    shape = jax.ShapeDtypeStruct((rows, 8 * lanes), jnp.bfloat16)
    return on_vmem(whole_kernel, 9, (), shape, (*mine, *theirs, *terms))


Y_SWAP = [(i, i ^ 1) for i in range(8)]
PAIR = [(0, 1), (1, 0)]


NEAR_SWAP = [(i, i ^ 2) for i in range(8)]
FAR_SWAP = [(i, i ^ 4) for i in range(8)]


def staged(gate_act, up_act, down_weight):
    batch = lax.axis_index("batch")
    depth, _, width = down_weight.shape
    w2 = down_weight.reshape(depth * 8, width)
    own = gated(gate_act, up_act)
    peer = lax.ppermute(own, "batch", PAIR)
    n_rows = own.shape[0]

    def over_y(outward):
        return lax.ppermute(outward, "mp", Y_SWAP)

    last, waited = [], []

    def step(function, *args):
        result = function(*args, tuple(last + waited))
        waited.clear()
        last[:] = list(result[:1]) if isinstance(result, (list, tuple)) else [result]
        return result

    def first(kept, got, pairs=NEAR_SWAP):
        sent, kept = step(combine, kept, got)
        return kept, lax.ppermute(sent, "mp", pairs)

    def far(terms):
        sent, kept = step(merge, *terms)
        return kept, lax.ppermute(sent, "mp", FAR_SWAP)

    def over_near(outward):
        return lax.ppermute(outward, "mp", NEAR_SWAP)

    def swap(x):
        return lax.ppermute(x, "batch", PAIR)

    def keeping(hids, chunk, pairs, after=()):
        return products(hids, w2, chunk, pairs, after, 4 if len(hids) == 1 else 2)

    both, near_first = [own, peer], (0, 2, 1, 3)
    a_out, w_0 = keeping([own], 0, (0, 1))
    last[:] = [a_out]
    a_got = over_y(a_out)
    d_out, w_1 = step(keeping, both, 1, (0, 1))
    d_got = over_y(d_out)
    c_out, c_kept, a_kept = step(dots, [peer, own], w_0, near_first, (2, 3))
    c_got = over_near(c_out)
    a = first(a_kept, a_got)
    e_out, w_2 = step(keeping, both, 2, (0, 1))
    e_got = over_y(e_out)
    (d_kept,) = step(dots, both, w_1, (0, 1), ())
    d = first(d_kept, d_got)
    a = far(a)
    (e_kept,) = step(dots, both, w_2, (0, 1), ())
    f_out, f_kept, w_3 = step(keeping, [peer], 3, (0, 1, 2, 3))
    f_got = over_y(f_out)
    d = far(d)
    e = first(e_kept, e_got)
    c = first(c_kept, c_got, Y_SWAP)
    (a,) = step(total, a, 1)
    g_out, g_kept = step(dots, [own], w_3, (0, 1, 2, 3), ())
    g_got = over_y(g_out)
    e = far(e)
    f = first(f_kept, f_got)
    c = far(c)
    d_mine, d_theirs = step(total, d, 2)
    given = [swap(d_theirs)]
    g = first(g_kept, g_got)
    waited.extend(given)
    f = far(f)
    (c,) = step(total, c, 1)
    given.append(swap(c))
    e_mine, e_theirs = step(total, e, 2)
    given.append(swap(e_theirs))
    g = far(g)
    (f,) = step(total, f, 1)
    d_got, c_got, e_got = given
    return whole((a, d_mine, e_mine), [c_got, d_got, e_got, swap(f)], g)


def general(gate_act, up_act, down_weight):
    hidden = gated(gate_act, up_act)
    piece = lax.all_gather(down_weight, "batch", axis=2, tiled=True)
    flat = piece.reshape(piece.shape[0], -1)
    result = jnp.dot(hidden, flat, preferred_element_type=jnp.float32)
    summed = lax.psum_scatter(result, "mp", scatter_dimension=1, tiled=True)
    return summed.astype(jnp.bfloat16)


def solution(mesh):
    def local(gate_act, up_act, down_weight):
        depth, blocks, width = down_weight.shape
        fits = (
            mesh.shape["mp"] == 8 and blocks == 8 and mesh.shape["batch"] == 2 and width == 4 * LANES
            and depth * 8 % (2 * SLAB * SORT_STEPS) == 0
        )
        return (staged if fits else general)(gate_act, up_act, down_weight)

    placed = (P(("groups", "batch"), "mp"), P(("groups", "batch"), "mp"), P("mp", None, "batch"))
    return jax.shard_map(
        local, mesh=mesh, in_specs=placed, out_specs=P(("groups", "batch"), "mp"), check_vma=False
    )
```

```python
import functools

import jax
import jax.numpy as jnp
from jax import lax
from jax.experimental import pallas as pl
from jax.experimental.pallas import tpu as pltpu
from jax.sharding import PartitionSpec as P

LANES = 128
SLAB = 256
SORT_STEPS = 4
BIG_STEP = pl.CostEstimate(flops=10_000_000_000, bytes_accessed=1024, transcendentals=0)
SMALL_STEP = pl.CostEstimate(flops=10_000_000_000, bytes_accessed=1024, transcendentals=0)
VMEM_LIMIT = 30 * 1024 * 1024


def gated(gate_act, up_act):
    return (jax.nn.silu(gate_act.astype(jnp.float32)) * up_act.astype(jnp.float32)).astype(
        jnp.bfloat16
    )


def product_kernel(n_hid, pairs, n_after, keep, split, w_ref, *refs):
    hid_refs, refs = refs[:n_hid], refs[n_hid + n_after:]
    out_refs, (order, w_sorted, hid, sems) = refs[:-4], refs[-4:]
    step = pl.program_id(0)
    slabs = w_ref.shape[0] // SLAB
    rows = hid_refs[0].shape[0]
    per = SLAB // 8
    n_sorted = w_sorted.shape[0]

    def copies():
        return [
            pltpu.make_async_copy(h, hid.at[pl.ds(n * rows, rows)], sems.at[n]) for n, h in enumerate(hid_refs)
        ]

    def keeping():
        return pltpu.make_async_copy(w_sorted.at[pl.ds(4 - keep, keep)], out_refs[-1], sems.at[n_hid])

    @pl.when(step == 0)
    def _():
        for c in copies():
            c.start()
        me = lax.axis_index("mp")
        to = lax.broadcasted_iota(jnp.int32, (SLAB, SLAB), 0)
        at = lax.broadcasted_iota(jnp.int32, (SLAB, SLAB), 1)
        block = at % 8
        far, near = (block // 4 + me // 4) % 2, (block // 2 + me // 2 + 1) % 2
        place = ((block % 2 + me + 1) % 2) * 4 + near * 2 + far
        same = jnp.logical_and(to % per == at // 8, to // per == place)
        order[...] = jnp.where(same, 1.0, 0.0).astype(jnp.bfloat16)

    @pl.when(step < SORT_STEPS)
    def _():
        for s in range(0, slabs, 2):
            two = jnp.concatenate(
                [w_ref[s * SLAB:(s + 1) * SLAB, :], w_ref[(s + 1) * SLAB:(s + 2) * SLAB, :]], axis=1
            )
            t = jnp.dot(order[...], two, preferred_element_type=jnp.float32).astype(jnp.bfloat16)
            for half in range(2):
                base = pl.multiple_of((step * slabs + s + half) * per, per)
                for i in range(8):
                    w_sorted[i // 2, pl.ds(base, per), (i % 2) * LANES:(i % 2 + 1) * LANES] = t[
                        i * per:(i + 1) * per, half * LANES:(half + 1) * LANES
                    ]

    @pl.when(step == SORT_STEPS)
    def _():
        keeping().start()
        for c in copies():
            c.wait()

    for n, p in enumerate(pairs):
        @pl.when(step == SORT_STEPS + n)
        def _(n=n, p=p):
            t = jnp.dot(hid[...], w_sorted[p], preferred_element_type=jnp.float32).astype(jnp.bfloat16)
            size = n_hid * rows // split
            for part in range(split):
                for side in range(2):
                    out_refs[n // 2 * split + part][side] = t[
                        part * size:(part + 1) * size, side * LANES:(side + 1) * LANES
                    ]
            if n == len(pairs) - 1:
                keeping().wait()


def products(hids, w2, chunk, pairs, after=(), keep=4, split=1):
    rows = hids[0].shape[0] * len(hids)
    depth = w2.shape[0] // 8
    n_out = len(pairs) // 2

    def out_map(o):
        return lambda s: (jnp.clip(s - SORT_STEPS - 2 * o, 0, 1), 0, 0)

    kept = jax.ShapeDtypeStruct((keep, depth, 2 * LANES), jnp.bfloat16)
    return pl.pallas_call(
        functools.partial(product_kernel, len(hids), pairs, len(after), keep, split),
        grid=(SORT_STEPS + len(pairs),),
        in_specs=[pl.BlockSpec((depth * 8 // SORT_STEPS, LANES), lambda s: (jnp.minimum(s, SORT_STEPS - 1), chunk))]
        + [pl.BlockSpec(memory_space=pl.ANY)] * (len(hids) + len(after)),
        out_specs=[pl.BlockSpec((2, rows // split, LANES), out_map(o)) for o in range(n_out) for _ in range(split)]
        + [pl.BlockSpec(memory_space=pltpu.HBM)],
        out_shape=[jax.ShapeDtypeStruct((4, rows // split, LANES), jnp.bfloat16)] * (n_out * split) + [kept],
        scratch_shapes=[
            pltpu.VMEM((SLAB, SLAB), jnp.bfloat16),
            pltpu.VMEM((4, depth, 2 * LANES), jnp.bfloat16),
            pltpu.VMEM((rows, depth), jnp.bfloat16),
            pltpu.SemaphoreType.DMA((len(hids) + 1,)),
        ],
        compiler_params=pltpu.CompilerParams(vmem_limit_bytes=VMEM_LIMIT),
        cost_estimate=BIG_STEP,
    )(w2, *hids, *after)


def dots_kernel(n_hid, pairs, extra, y_first, split, n_after, *refs):
    hid_refs, w_ref, refs = refs[:n_hid], refs[n_hid], refs[n_hid + 1 + n_after:]
    out_refs, (w_held, sems) = refs[:-2], refs[-2:]
    step = pl.program_id(0)
    rows = hid_refs[0].shape[0]

    def copy(n):
        return pltpu.make_async_copy(w_ref.at[pairs[n]], w_held.at[n % 2], sems.at[n % 2])

    def put(hid, n, out, at):
        t = jnp.dot(hid[...], w_held[n % 2], preferred_element_type=jnp.float32).astype(jnp.bfloat16)
        for side in range(2):
            out[side, at:at + rows] = t[:, side * LANES:(side + 1) * LANES]

    for n in range(len(pairs)):
        @pl.when(step == n)
        def _(n=n):
            if n == 0:
                copy(0).start()
            if n + 1 < len(pairs):
                copy(n + 1).start()
            copy(n).wait()
            for h, hid in enumerate(hid_refs):
                if split > 1:
                    put(hid, n, out_refs[n // 2 * split + h], 0)
                elif h == 0 or not extra:
                    put(hid, n, out_refs[pairs[n] // 2 if y_first else n // 2], h * rows)
                elif pairs[n] in extra:
                    put(hid, n, out_refs[-1], 0)


def dots(hids, w_sorted, pairs, extra=(), y_first=False, split=1, after=()):
    rows, depth = hids[0].shape
    n_out = len(pairs) // 2
    out_rows = rows if extra else rows * len(hids) // split

    def out_map(o):
        return lambda s: (jnp.clip(s - 2 * o, 0, 1), 0, 0)

    halves = [lambda s: (s // 2, 0, 0)]
    maps = (halves * n_out if y_first else [out_map(o) for o in range(n_out) for _ in range(split)]) + halves * bool(extra)
    return pl.pallas_call(
        functools.partial(dots_kernel, len(hids), pairs, extra, y_first, split, len(after)),
        grid=(len(pairs),),
        in_specs=[pl.BlockSpec((rows, depth), lambda s: (0, 0))] * len(hids) + [pl.BlockSpec(memory_space=pltpu.HBM)]
        + [pl.BlockSpec(memory_space=pl.ANY)] * len(after),
        out_specs=[pl.BlockSpec((2, out_rows, LANES), m) for m in maps],
        out_shape=[jax.ShapeDtypeStruct((4, out_rows, LANES), jnp.bfloat16)] * len(maps),
        scratch_shapes=[pltpu.VMEM((2, depth, 2 * LANES), jnp.bfloat16), pltpu.SemaphoreType.DMA((2,))],
        compiler_params=pltpu.CompilerParams(vmem_limit_bytes=VMEM_LIMIT),
        cost_estimate=BIG_STEP,
    )(*hids, w_sorted, *after)


def on_vmem(kernel, n_in, after, out_shape, args):
    vmem = pl.BlockSpec(memory_space=pltpu.VMEM)
    many = isinstance(out_shape, list)
    return pl.pallas_call(
        kernel,
        in_specs=[vmem] * n_in + [pl.BlockSpec(memory_space=pl.ANY)] * len(after),
        out_specs=[vmem] * len(out_shape) if many else vmem,
        out_shape=out_shape,
        compiler_params=pltpu.CompilerParams(vmem_limit_bytes=12 * 1024 * 1024),
        cost_estimate=SMALL_STEP,
    )(*args, *after)


def summed(*refs):
    return sum(r[...].astype(jnp.float32) for r in refs)


def combine_kernel(n_after, own_ref, got_ref, *refs):
    sent, kept = refs[n_after:]
    for i in range(2):
        sent[i] = summed(own_ref.at[i], got_ref.at[i]).astype(jnp.bfloat16)
        kept[i] = summed(own_ref.at[2 + i], got_ref.at[2 + i])


def combine(own, got, after=()):
    _, rows, lanes = own.shape
    shape = [jax.ShapeDtypeStruct((2, rows, lanes), d) for d in (jnp.bfloat16, jnp.float32)]
    return on_vmem(functools.partial(combine_kernel, len(after)), 2, after, shape, (own, got))


def merge_kernel(n_after, own_ref, got_ref, *refs):
    sent, kept = refs[n_after:]
    sent[...] = summed(own_ref.at[1], got_ref.at[1]).astype(jnp.bfloat16)
    kept[...] = summed(own_ref.at[0], got_ref.at[0])


def merge(own, got, after=()):
    _, rows, lanes = own.shape
    shape = [jax.ShapeDtypeStruct((rows, lanes), d) for d in (jnp.bfloat16, jnp.float32)]
    return on_vmem(functools.partial(merge_kernel, len(after)), 2, after, shape, (own, got))


def total_kernel(n_after, parts, own_ref, got_ref, *refs):
    outs = refs[n_after:]
    rows = outs[0].shape[0]
    for p in range(parts):
        at = pl.ds(p * rows, rows)
        outs[p][...] = summed(own_ref.at[at], got_ref.at[at]).astype(jnp.bfloat16)


def total(terms, parts, after=()):
    rows, lanes = terms[0].shape
    shape = [jax.ShapeDtypeStruct((rows // parts, lanes), jnp.bfloat16)] * parts
    return on_vmem(functools.partial(total_kernel, len(after), parts), 2, after, shape, terms)


def whole_kernel(*refs):
    out, mine, theirs, terms = refs[-1], refs[:3], refs[3:7], refs[7:9]
    batch = lax.axis_index("batch")

    for b in range(2):
        @pl.when(batch == b)
        def _(b=b):
            def put(half, n, value):
                out[:, (half * 4 + n) * LANES:(half * 4 + n + 1) * LANES] = value

            for n in range(3):
                put(b, n, mine[n][...])
            put(b, 3, summed(*terms).astype(jnp.bfloat16))
            for n in range(4):
                put(1 - b, n, theirs[n][...])


def whole(mine, theirs, terms):
    rows, lanes = mine[0].shape
    shape = jax.ShapeDtypeStruct((rows, 8 * lanes), jnp.bfloat16)
    return on_vmem(whole_kernel, 9, (), shape, (*mine, *theirs, *terms))


Y_SWAP = [(i, i ^ 1) for i in range(8)]
PAIR = [(0, 1), (1, 0)]


NEAR_SWAP = [(i, i ^ 2) for i in range(8)]
FAR_SWAP = [(i, i ^ 4) for i in range(8)]


def staged(gate_act, up_act, down_weight):
    batch = lax.axis_index("batch")
    depth, _, width = down_weight.shape
    w2 = down_weight.reshape(depth * 8, width)
    own = gated(gate_act, up_act)
    peer = lax.ppermute(own, "batch", PAIR)
    n_rows = own.shape[0]

    def over_y(outward):
        return lax.ppermute(outward, "mp", Y_SWAP)

    last, waited = [], []

    def step(function, *args):
        result = function(*args, tuple(last + waited))
        waited.clear()
        last[:] = list(result[:1]) if isinstance(result, (list, tuple)) else [result]
        return result

    def first(kept, got, pairs=NEAR_SWAP):
        sent, kept = step(combine, kept, got)
        return kept, lax.ppermute(sent, "mp", pairs)

    def far(terms):
        sent, kept = step(merge, *terms)
        return kept, lax.ppermute(sent, "mp", FAR_SWAP)

    def over_near(outward):
        return lax.ppermute(outward, "mp", NEAR_SWAP)

    def swap(x):
        return lax.ppermute(x, "batch", PAIR)

    def keeping(hids, chunk, pairs, split=1, after=()):
        return products(hids, w2, chunk, pairs, after, 4 if len(hids) == 1 else 2, split)

    both, near_first = [own, peer], (0, 2, 1, 3)
    a_out, w_0 = keeping([own], 0, (0, 1))
    last[:] = [a_out]
    a_got = over_y(a_out)
    d_out, w_1 = step(keeping, both, 1, (0, 1), 1)
    d_got = over_y(d_out)
    c_out, c_kept, a_kept = step(dots, [peer, own], w_0, near_first, (2, 3), False, 1)
    c_got = over_near(c_out)
    a = first(a_kept, a_got)
    e_out, b_out, w_2 = step(keeping, both, 2, (0, 1), 2)
    b_got = over_y(b_out)
    e_got = over_y(e_out)
    (d_kept,) = step(dots, both, w_1, (0, 1), (), False, 1)
    d = first(d_kept, d_got)
    a = far(a)
    e_kept, b_kept = step(dots, both, w_2, (0, 1), (), False, 2)
    b = first(b_kept, b_got)
    f_out, w_3 = step(keeping, [peer], 3, (0, 1), 1)
    f_got = over_y(f_out)
    (a,) = step(total, a, 1)
    d = far(d)
    e = first(e_kept, e_got)
    c = first(c_kept, c_got, Y_SWAP)
    b = far(b)
    g_out, g_kept, f_kept = step(dots, [own, peer], w_3, near_first, (2, 3), True, 1)
    g_got = over_y(g_out)
    d_mine, d_theirs = step(total, d, 2)
    d_got = swap(d_theirs)
    e = far(e)
    f = first(f_kept, f_got)
    c = far(c)
    (b,) = step(total, b, 1)
    b_got = swap(b)
    waited.extend([d_got])
    g = first(g_kept, g_got)
    f = far(f)
    (c,) = step(total, c, 1)
    c_got = swap(c)
    (e,) = step(total, e, 1)
    waited.extend([b_got])
    g = far(g)
    (f,) = step(total, f, 1)
    return whole((a, d_mine, e), [c_got, d_got, b_got, swap(f)], g)


def general(gate_act, up_act, down_weight):
    hidden = gated(gate_act, up_act)
    piece = lax.all_gather(down_weight, "batch", axis=2, tiled=True)
    flat = piece.reshape(piece.shape[0], -1)
    result = jnp.dot(hidden, flat, preferred_element_type=jnp.float32)
    summed = lax.psum_scatter(result, "mp", scatter_dimension=1, tiled=True)
    return summed.astype(jnp.bfloat16)


def solution(mesh):
    def local(gate_act, up_act, down_weight):
        depth, blocks, width = down_weight.shape
        fits = (
            mesh.shape["mp"] == 8 and blocks == 8 and mesh.shape["batch"] == 2 and width == 4 * LANES
            and depth * 8 % (2 * SLAB * SORT_STEPS) == 0
        )
        return (staged if fits else general)(gate_act, up_act, down_weight)

    placed = (P(("groups", "batch"), "mp"), P(("groups", "batch"), "mp"), P("mp", None, "batch"))
    return jax.shard_map(
        local, mesh=mesh, in_specs=placed, out_specs=P(("groups", "batch"), "mp"), check_vma=False
    )
```

```python
import functools

import jax
import jax.numpy as jnp
from jax import lax
from jax.experimental import pallas as pl
from jax.experimental.pallas import tpu as pltpu
from jax.sharding import PartitionSpec as P

LANES = 128
SLAB = 256
SORT_STEPS = 4
BIG_STEP = pl.CostEstimate(flops=10_000_000_000, bytes_accessed=1024, transcendentals=0)
SMALL_STEP = pl.CostEstimate(flops=10_000_000_000, bytes_accessed=1024, transcendentals=0)
VMEM_LIMIT = 30 * 1024 * 1024


def gated(gate_act, up_act):
    return (jax.nn.silu(gate_act.astype(jnp.float32)) * up_act.astype(jnp.float32)).astype(
        jnp.bfloat16
    )


def product_kernel(n_hid, pairs, n_after, keep, split, w_ref, *refs):
    hid_refs, refs = refs[:n_hid], refs[n_hid + n_after:]
    out_refs, (order, w_sorted, hid, sems) = refs[:-4], refs[-4:]
    step = pl.program_id(0)
    slabs = w_ref.shape[0] // SLAB
    rows = hid_refs[0].shape[0]
    per = SLAB // 8
    n_sorted = w_sorted.shape[0]

    def copies():
        return [
            pltpu.make_async_copy(h, hid.at[pl.ds(n * rows, rows)], sems.at[n]) for n, h in enumerate(hid_refs)
        ]

    def keeping():
        return pltpu.make_async_copy(w_sorted.at[pl.ds(4 - keep, keep)], out_refs[-1], sems.at[n_hid])

    @pl.when(step == 0)
    def _():
        for c in copies():
            c.start()
        me = lax.axis_index("mp")
        to = lax.broadcasted_iota(jnp.int32, (SLAB, SLAB), 0)
        at = lax.broadcasted_iota(jnp.int32, (SLAB, SLAB), 1)
        block = at % 8
        far, near = (block // 4 + me // 4) % 2, (block // 2 + me // 2 + 1) % 2
        place = ((block % 2 + me + 1) % 2) * 4 + near * 2 + far
        same = jnp.logical_and(to % per == at // 8, to // per == place)
        order[...] = jnp.where(same, 1.0, 0.0).astype(jnp.bfloat16)

    @pl.when(step < SORT_STEPS)
    def _():
        for s in range(0, slabs, 2):
            two = jnp.concatenate(
                [w_ref[s * SLAB:(s + 1) * SLAB, :], w_ref[(s + 1) * SLAB:(s + 2) * SLAB, :]], axis=1
            )
            t = jnp.dot(order[...], two, preferred_element_type=jnp.float32).astype(jnp.bfloat16)
            for half in range(2):
                base = pl.multiple_of((step * slabs + s + half) * per, per)
                for i in range(8):
                    w_sorted[i // 2, pl.ds(base, per), (i % 2) * LANES:(i % 2 + 1) * LANES] = t[
                        i * per:(i + 1) * per, half * LANES:(half + 1) * LANES
                    ]

    @pl.when(step == SORT_STEPS)
    def _():
        keeping().start()
        for c in copies():
            c.wait()

    for n, p in enumerate(pairs):
        @pl.when(step == SORT_STEPS + n)
        def _(n=n, p=p):
            t = jnp.dot(hid[...], w_sorted[p], preferred_element_type=jnp.float32).astype(jnp.bfloat16)
            size = n_hid * rows // split
            for part in range(split):
                for side in range(2):
                    out_refs[n // 2 * split + part][side] = t[
                        part * size:(part + 1) * size, side * LANES:(side + 1) * LANES
                    ]
            if n == len(pairs) - 1:
                keeping().wait()


def products(hids, w2, chunk, pairs, after=(), keep=4, split=1):
    rows = hids[0].shape[0] * len(hids)
    depth = w2.shape[0] // 8
    n_out = len(pairs) // 2

    def out_map(o):
        return lambda s: (jnp.clip(s - SORT_STEPS - 2 * o, 0, 1), 0, 0)

    kept = jax.ShapeDtypeStruct((keep, depth, 2 * LANES), jnp.bfloat16)
    return pl.pallas_call(
        functools.partial(product_kernel, len(hids), pairs, len(after), keep, split),
        grid=(SORT_STEPS + len(pairs),),
        in_specs=[pl.BlockSpec((depth * 8 // SORT_STEPS, LANES), lambda s: (jnp.minimum(s, SORT_STEPS - 1), chunk))]
        + [pl.BlockSpec(memory_space=pl.ANY)] * (len(hids) + len(after)),
        out_specs=[pl.BlockSpec((2, rows // split, LANES), out_map(o)) for o in range(n_out) for _ in range(split)]
        + [pl.BlockSpec(memory_space=pltpu.HBM)],
        out_shape=[jax.ShapeDtypeStruct((4, rows // split, LANES), jnp.bfloat16)] * (n_out * split) + [kept],
        scratch_shapes=[
            pltpu.VMEM((SLAB, SLAB), jnp.bfloat16),
            pltpu.VMEM((4, depth, 2 * LANES), jnp.bfloat16),
            pltpu.VMEM((rows, depth), jnp.bfloat16),
            pltpu.SemaphoreType.DMA((len(hids) + 1,)),
        ],
        compiler_params=pltpu.CompilerParams(vmem_limit_bytes=VMEM_LIMIT),
        cost_estimate=BIG_STEP,
    )(w2, *hids, *after)


def dots_kernel(n_hid, pairs, extra, y_first, split, n_after, *refs):
    hid_refs, w_ref, refs = refs[:n_hid], refs[n_hid], refs[n_hid + 1 + n_after:]
    out_refs, (w_held, sems) = refs[:-2], refs[-2:]
    step = pl.program_id(0)
    rows = hid_refs[0].shape[0]

    def copy(n):
        return pltpu.make_async_copy(w_ref.at[pairs[n]], w_held.at[n % 2], sems.at[n % 2])

    def put(hid, n, out, at):
        t = jnp.dot(hid[...], w_held[n % 2], preferred_element_type=jnp.float32).astype(jnp.bfloat16)
        for side in range(2):
            out[side, at:at + rows] = t[:, side * LANES:(side + 1) * LANES]

    for n in range(len(pairs)):
        @pl.when(step == n)
        def _(n=n):
            if n == 0:
                copy(0).start()
            if n + 1 < len(pairs):
                copy(n + 1).start()
            copy(n).wait()
            for h, hid in enumerate(hid_refs):
                if split > 1:
                    put(hid, n, out_refs[n // 2 * split + h], 0)
                elif h == 0 or not extra:
                    put(hid, n, out_refs[pairs[n] // 2 if y_first else n // 2], h * rows)
                elif pairs[n] in extra:
                    put(hid, n, out_refs[-1], 0)


def dots(hids, w_sorted, pairs, extra=(), y_first=False, split=1, after=()):
    rows, depth = hids[0].shape
    n_out = len(pairs) // 2
    out_rows = rows if extra else rows * len(hids) // split

    def out_map(o):
        return lambda s: (jnp.clip(s - 2 * o, 0, 1), 0, 0)

    halves = [lambda s: (s // 2, 0, 0)]
    maps = (halves * n_out if y_first else [out_map(o) for o in range(n_out) for _ in range(split)]) + halves * bool(extra)
    return pl.pallas_call(
        functools.partial(dots_kernel, len(hids), pairs, extra, y_first, split, len(after)),
        grid=(len(pairs),),
        in_specs=[pl.BlockSpec((rows, depth), lambda s: (0, 0))] * len(hids) + [pl.BlockSpec(memory_space=pltpu.HBM)]
        + [pl.BlockSpec(memory_space=pl.ANY)] * len(after),
        out_specs=[pl.BlockSpec((2, out_rows, LANES), m) for m in maps],
        out_shape=[jax.ShapeDtypeStruct((4, out_rows, LANES), jnp.bfloat16)] * len(maps),
        scratch_shapes=[pltpu.VMEM((2, depth, 2 * LANES), jnp.bfloat16), pltpu.SemaphoreType.DMA((2,))],
        compiler_params=pltpu.CompilerParams(vmem_limit_bytes=VMEM_LIMIT),
        cost_estimate=BIG_STEP,
    )(*hids, w_sorted, *after)


def on_vmem(kernel, n_in, after, out_shape, args):
    vmem = pl.BlockSpec(memory_space=pltpu.VMEM)
    many = isinstance(out_shape, list)
    return pl.pallas_call(
        kernel,
        in_specs=[vmem] * n_in + [pl.BlockSpec(memory_space=pl.ANY)] * len(after),
        out_specs=[vmem] * len(out_shape) if many else vmem,
        out_shape=out_shape,
        compiler_params=pltpu.CompilerParams(vmem_limit_bytes=12 * 1024 * 1024),
        cost_estimate=SMALL_STEP,
    )(*args, *after)


def summed(*refs):
    return sum(r[...].astype(jnp.float32) for r in refs)


def combine_kernel(n_after, own_ref, got_ref, *refs):
    sent, kept = refs[n_after:]
    for i in range(2):
        sent[i] = summed(own_ref.at[i], got_ref.at[i]).astype(jnp.bfloat16)
        kept[i] = summed(own_ref.at[2 + i], got_ref.at[2 + i])


def combine(own, got, after=()):
    _, rows, lanes = own.shape
    shape = [jax.ShapeDtypeStruct((2, rows, lanes), d) for d in (jnp.bfloat16, jnp.float32)]
    return on_vmem(functools.partial(combine_kernel, len(after)), 2, after, shape, (own, got))


def merge_kernel(n_after, own_ref, got_ref, *refs):
    sent, kept = refs[n_after:]
    sent[...] = summed(own_ref.at[1], got_ref.at[1]).astype(jnp.bfloat16)
    kept[...] = summed(own_ref.at[0], got_ref.at[0])


def merge(own, got, after=()):
    _, rows, lanes = own.shape
    shape = [jax.ShapeDtypeStruct((rows, lanes), d) for d in (jnp.bfloat16, jnp.float32)]
    return on_vmem(functools.partial(merge_kernel, len(after)), 2, after, shape, (own, got))


def total_kernel(n_after, parts, own_ref, got_ref, *refs):
    outs = refs[n_after:]
    rows = outs[0].shape[0]
    for p in range(parts):
        at = pl.ds(p * rows, rows)
        outs[p][...] = summed(own_ref.at[at], got_ref.at[at]).astype(jnp.bfloat16)


def total(terms, parts, after=()):
    rows, lanes = terms[0].shape
    shape = [jax.ShapeDtypeStruct((rows // parts, lanes), jnp.bfloat16)] * parts
    return on_vmem(functools.partial(total_kernel, len(after), parts), 2, after, shape, terms)


def whole_kernel(*refs):
    out, mine, theirs, terms = refs[-1], refs[:3], refs[3:7], refs[7:9]
    batch = lax.axis_index("batch")

    for b in range(2):
        @pl.when(batch == b)
        def _(b=b):
            def put(half, n, value):
                out[:, (half * 4 + n) * LANES:(half * 4 + n + 1) * LANES] = value

            for n in range(3):
                put(b, n, mine[n][...])
            put(b, 3, summed(*terms).astype(jnp.bfloat16))
            for n in range(4):
                put(1 - b, n, theirs[n][...])


def whole(mine, theirs, terms):
    rows, lanes = mine[0].shape
    shape = jax.ShapeDtypeStruct((rows, 8 * lanes), jnp.bfloat16)
    return on_vmem(whole_kernel, 9, (), shape, (*mine, *theirs, *terms))


Y_SWAP = [(i, i ^ 1) for i in range(8)]
PAIR = [(0, 1), (1, 0)]


NEAR_SWAP = [(i, i ^ 2) for i in range(8)]
FAR_SWAP = [(i, i ^ 4) for i in range(8)]


def staged(gate_act, up_act, down_weight):
    batch = lax.axis_index("batch")
    depth, _, width = down_weight.shape
    w2 = down_weight.reshape(depth * 8, width)
    own = gated(gate_act, up_act)
    peer = lax.ppermute(own, "batch", PAIR)
    n_rows = own.shape[0]

    def over_y(outward):
        return lax.ppermute(outward, "mp", Y_SWAP)

    last, waited = [], []

    def step(function, *args):
        result = function(*args, tuple(last + waited))
        waited.clear()
        last[:] = list(result[:1]) if isinstance(result, (list, tuple)) else [result]
        return result

    def first(kept, got, pairs=NEAR_SWAP):
        sent, kept = step(combine, kept, got)
        return kept, lax.ppermute(sent, "mp", pairs)

    def far(terms):
        sent, kept = step(merge, *terms)
        return kept, lax.ppermute(sent, "mp", FAR_SWAP)

    def over_near(outward):
        return lax.ppermute(outward, "mp", NEAR_SWAP)

    def swap(x):
        return lax.ppermute(x, "batch", PAIR)

    def keeping(hids, chunk, pairs, split=1, after=()):
        return products(hids, w2, chunk, pairs, after, 4 if len(hids) == 1 else 2, split)

    both, near_first = [own, peer], (0, 2, 1, 3)
    a_out, w_0 = keeping([own], 0, (0, 1))
    last[:] = [a_out]
    a_got = over_y(a_out)
    d_out, w_1 = step(keeping, both, 1, (0, 1), 1)
    d_got = over_y(d_out)
    c_out, c_kept, a_kept = step(dots, [peer, own], w_0, near_first, (2, 3), False, 1)
    c_got = over_near(c_out)
    a = first(a_kept, a_got)
    e_out, b_out, w_2 = step(keeping, both, 2, (0, 1), 2)
    b_got = over_y(b_out)
    e_got = over_y(e_out)
    (d_kept,) = step(dots, both, w_1, (0, 1), (), False, 1)
    d = first(d_kept, d_got)
    a = far(a)
    e_kept, b_kept = step(dots, both, w_2, (0, 1), (), False, 2)
    b = first(b_kept, b_got)
    f_out, w_3 = step(keeping, [peer], 3, (0, 1), 1)
    f_got = over_y(f_out)
    (a,) = step(total, a, 1)
    d = far(d)
    e = first(e_kept, e_got)
    b = far(b)
    g_out, g_kept, f_kept = step(dots, [own, peer], w_3, near_first, (2, 3), True, 1)
    g_got = over_y(g_out)
    c = first(c_kept, c_got, Y_SWAP)
    d_mine, d_theirs = step(total, d, 2)
    d_got = swap(d_theirs)
    e = far(e)
    f = first(f_kept, f_got)
    (b,) = step(total, b, 1)
    b_got = swap(b)
    waited.extend([d_got])
    g = first(g_kept, g_got)
    c = far(c)
    f = far(f)
    (c,) = step(total, c, 1)
    c_got = swap(c)
    (e,) = step(total, e, 1)
    waited.extend([b_got])
    g = far(g)
    (f,) = step(total, f, 1)
    return whole((a, d_mine, e), [c_got, d_got, b_got, swap(f)], g)


def general(gate_act, up_act, down_weight):
    hidden = gated(gate_act, up_act)
    piece = lax.all_gather(down_weight, "batch", axis=2, tiled=True)
    flat = piece.reshape(piece.shape[0], -1)
    result = jnp.dot(hidden, flat, preferred_element_type=jnp.float32)
    summed = lax.psum_scatter(result, "mp", scatter_dimension=1, tiled=True)
    return summed.astype(jnp.bfloat16)


def solution(mesh):
    def local(gate_act, up_act, down_weight):
        depth, blocks, width = down_weight.shape
        fits = (
            mesh.shape["mp"] == 8 and blocks == 8 and mesh.shape["batch"] == 2 and width == 4 * LANES
            and depth * 8 % (2 * SLAB * SORT_STEPS) == 0
        )
        return (staged if fits else general)(gate_act, up_act, down_weight)

    placed = (P(("groups", "batch"), "mp"), P(("groups", "batch"), "mp"), P("mp", None, "batch"))
    return jax.shard_map(
        local, mesh=mesh, in_specs=placed, out_specs=P(("groups", "batch"), "mp"), check_vma=False
    )
```
